256 devices in a mesh: win: 32 (over x, z), pair: 8 (over y, core).
Axes of the slice: x: 4, y: 4, z: 8, core: 2. Of those that a mesh axis runs over, the one named last changes fastest.
Arguments:
- raw_strain: bfloat16 [64, 8256, 2048], P('win', None, 'pair'), may hold values from -80 to 80
- fir_taps: float32 [64], replicated, may hold values from -0.75 to 0.75
- block_tiles: int32 [32, 2], P('pair'), may hold values from 0 to 15, as said below
- block_count: int32 [8], P('pair'), may hold values from 2 to 4, as said below
Outputs:
- correlations: float32 [256, 32, 2048], P('win', 'pair')
The draws below stay inside these ranges and needn't reach their ends.
Inputs may be any that keep to these rules, and one draw needn't show every extreme that they name: `block_tiles`: rows come in groups of 4, one group for each index of pair in order. Column 1 names a tile held by that index (tiles o * 2 to (o + 1) * 2 - 1 for group o), and the group's first 2 rows name these tiles in order. Column 0 names a tile a with |a - b| <= 2, where b is column 1. In the group's first row a = max(b - 2, 0), in its second row a = min(b + 2, 15). Only the first block_count[o] slots of group o are live; the rest are padding.
All inputs are finite; a program needn't handle non-finite values.
Results may differ from the reference program's by a relative error of at most 0.0065.
Values may be sent and summed in bfloat16 or wider, within the bound.
No kernel may reach another device: no remote copies, remote signals or barrier semaphores. Data moves between devices by JAX's collectives and lax.ppermute only.
A program may use at most 128 MiB of HBM per device.

```python
import math
import jax
import jax.numpy as jnp
from jax import lax

TILE_DEV = 2
TILE = 128
VS = 2
NS = 2048
TAPS = 64
STRIDE = 4
BAND = 64
F = 1024
NB = 16
LAGS = 2048
T_RAW = 8256
BLK_DEV = 4
PAIRS = 256
SUBS = 64
TILES = 16
CHANNELS = 2048
BLOCKS = 32
N_PAIR = 8


def draw_raw_strain(key, part):
    key = jax.random.fold_in(key, 11)
    first, second = jax.random.split(key, 2)
    gains = jnp.exp(jax.random.uniform(first, (1, 1, CHANNELS), jnp.float32, 0.0, math.log(10.0)))
    values = jax.random.normal(second, (SUBS, T_RAW, CHANNELS), jnp.float32)
    values = jnp.clip(values, -5.0, 5.0) * gains
    return values.astype(jnp.bfloat16)


def draw_block_tiles(key, part):
    key = jax.random.fold_in(key, 23)
    first, second = jax.random.split(key, 2)
    rows = jnp.arange(BLOCKS, dtype=jnp.int32)
    owner = rows // BLK_DEV
    within = rows % BLK_DEV
    picked = jax.random.randint(first, (BLOCKS,), 0, TILE_DEV, jnp.int32)
    local = jnp.where(within < TILE_DEV, within, picked)
    receiver = owner * TILE_DEV + local
    offset = jax.random.randint(second, (BLOCKS,), -2, 3, jnp.int32)
    offset = jnp.where(within == 0, -2, jnp.where(within == 1, 2, offset))
    source = jnp.clip(receiver + offset, 0, TILES - 1)
    return jnp.stack([source, receiver], axis=1).astype(jnp.int32)


def draw_block_count(key, part):
    key = jax.random.fold_in(key, 37)
    first, second = jax.random.split(key, 2)
    counts = jax.random.randint(first, (N_PAIR,), TILE_DEV, BLK_DEV + 1, jnp.int32)
    fullest = jax.random.randint(second, (), 0, N_PAIR, jnp.int32)
    marker = jnp.arange(N_PAIR, dtype=jnp.int32) == fullest
    return jnp.where(marker, BLK_DEV, counts).astype(jnp.int32)


def normal_values(stream_key, shape, deviation, bound, kind=jnp.bfloat16):
    result = deviation * jax.random.normal(stream_key, shape, jnp.float32)
    return jnp.clip(result, min=-bound, max=bound).astype(kind)


def setup_inputs(seed: int = 0) -> dict:
    seeds = jax.random.split(jax.random.key(seed), 5)
    raw_strain = draw_raw_strain(jax.random.fold_in(seeds[4], 71), 0)
    fir_taps = normal_values(seeds[1], (TAPS,), TAPS ** -0.5, 0.75, jnp.float32)
    block_tiles = draw_block_tiles(jax.random.fold_in(seeds[4], 71), 0)
    block_count = draw_block_count(jax.random.fold_in(seeds[4], 71), 0)
    return dict(raw_strain=raw_strain, fir_taps=fir_taps, block_tiles=block_tiles, block_count=block_count)


def dft_rows(length, bins):
    freq = jnp.arange(bins, dtype=jnp.int32)
    times = jnp.arange(length, dtype=jnp.int32)
    phase = freq[:, None] * times[None, :] % length
    angle = phase.astype(jnp.float32) * jnp.float32(2.0 * math.pi / length)
    return jnp.concatenate([jnp.cos(angle), -jnp.sin(angle)], axis=0).astype(jnp.bfloat16)

def lag_rows(length, bins, lags, total_subs):
    freq = jnp.arange(bins, dtype=jnp.int32)
    shift = jnp.arange(lags, dtype=jnp.int32) - lags // 2
    phase = freq[:, None] * shift[None, :] % length
    angle = phase.astype(jnp.float32) * jnp.float32(2.0 * math.pi / length)
    weight = jnp.where(freq == 0, 1.0, 2.0).astype(jnp.float32) / jnp.sqrt(jnp.float32(2.0 * bins * total_subs))
    return jnp.concatenate([weight[:, None] * jnp.cos(angle), -weight[:, None] * jnp.sin(angle)], axis=0)

def reference(raw_strain, fir_taps, block_tiles, block_count):
    table = dft_rows(NS, F).astype(jnp.float32)
    source_ids = block_tiles[:, 0]
    receiver_ids = block_tiles[:, 1]
    slots = jnp.arange(BLOCKS, dtype=jnp.int32)
    live = (slots % BLK_DEV < block_count[slots // BLK_DEV]).astype(jnp.float32)

    def one_window(carry, window):
        frames = window.reshape(NS + TAPS // STRIDE, STRIDE, CHANNELS)
        filtered = jnp.zeros((NS, CHANNELS), jnp.float32)
        for step in range(TAPS // STRIDE):
            taps = fir_taps[STRIDE * step:STRIDE * step + STRIDE]
            filtered = filtered + lax.optimization_barrier(jnp.sum(frames[step:step + NS].astype(jnp.float32) * taps[None, :, None], axis=1))
        filtered = filtered.astype(jnp.bfloat16)
        spectrum = jnp.dot(table, filtered.astype(jnp.float32), precision=lax.Precision.HIGHEST)
        banded = spectrum.reshape(2, NB, BAND, CHANNELS)
        power = lax.optimization_barrier(jnp.mean(banded * banded, axis=(0, 2)))
        whitened = (banded / jnp.sqrt(power + 1e-06)[None, :, None, :]).reshape(2 * F, CHANNELS)
        whitened = whitened.astype(jnp.bfloat16).astype(jnp.float32)
        sources = whitened.reshape(2 * F, TILES, VS, TILE // VS)[:, :, :, 0]
        left = sources[:, source_ids] * live[None, :, None]
        right = whitened.reshape(2 * F, TILES, TILE)[:, receiver_ids]
        left_re, left_im = (left[:F], left[F:])
        right_re, right_im = (right[:F], right[F:])
        real_part = left_re[:, :, :, None] * right_re[:, :, None, :] + left_im[:, :, :, None] * right_im[:, :, None, :]
        imag_part = left_re[:, :, :, None] * right_im[:, :, None, :] - left_im[:, :, :, None] * right_re[:, :, None, :]
        return (carry + jnp.stack([real_part, imag_part]), None)
    start = jnp.zeros((2, F, BLOCKS, VS, TILE), jnp.float32)
    summed, unused = lax.scan(one_window, start, raw_strain)
    cross = jnp.transpose(summed, (0, 3, 4, 2, 1)).reshape(2, PAIRS, BLOCKS, F)
    cross = jnp.concatenate([cross[0], cross[1]], axis=-1)
    lagged = lag_rows(NS, F, LAGS, SUBS)
    return jnp.einsum('pkf,fl->pkl', cross, lagged, precision=lax.Precision.HIGHEST)
```

```python
import functools

import jax
import jax.numpy as jnp
import ml_dtypes
import numpy as np
from jax import lax
from jax.experimental import pallas as pl
from jax.experimental.pallas import tpu as pltpu
from jax.sharding import PartitionSpec as P

TILE = 128
VS = 2
NS = 2048
TAPS = 64
STRIDE = 4
BAND = 64
F = 1024
LAGS = 2048
T_RAW = 8256
CH = 256
SLOTS = 4
SUBS_DEV = 2
WX = 4
WZ = 8
GROUP = 8
FG = F // GROUP
HALF = FG // 2
TILES = 4
FT = F // TILES
ROWS = 48
SPAN = 256
BLOCKS = -(-NS // ROWS)
T_PAD = (BLOCKS - 1) * STRIDE * ROWS + SPAN
ROLL = (128, 640)
SIZE = 2 * CH
PIECES = ((0, 2112), (2112, 2048), (4160, 2048), (6208, 2048))
F32 = jnp.float32
BF16 = jnp.bfloat16


def dft_table():
    freq = np.arange(F).reshape(TILES, 2, HALF, 2).transpose(0, 1, 3, 2)
    phase = freq[..., None] * np.arange(NS // 2) % NS
    angle = phase.astype(np.float32) * np.float32(2.0 * np.pi / NS)
    table = np.stack([np.cos(angle), -np.sin(angle)], axis=1)
    return table.astype(np.float32).astype(ml_dtypes.bfloat16)


def spectra_kernel(u, taps_hbm, raw_hbm, table_hbm, *refs):
    before = refs[:u]
    out, src_ref, raw, table, filt, src, taps_ref, row, sems = refs[u:]
    taps_copy = pltpu.make_async_copy(taps_hbm, taps_ref, sems.at[8])
    raw_copies = [
        pltpu.make_async_copy(raw_hbm.at[u, pl.ds(at, size)], raw.at[pl.ds(at, size)], sems.at[p])
        for p, (at, size) in enumerate(PIECES)
    ]
    table_copies = [
        pltpu.make_async_copy(table_hbm.at[t], table.at[t], sems.at[4 + t])
        for t in range(TILES)
    ]
    taps_copy.start()
    for copy in raw_copies + table_copies:
        copy.start()
    raw[T_RAW:, :] = jnp.zeros((T_PAD - T_RAW, CH), BF16)

    row[...] = jnp.zeros(row.shape, F32)
    taps_copy.wait()
    row[:, :TAPS] = taps_ref[...]
    taps = row[...]
    high = taps.astype(BF16).astype(F32)
    terms = []
    for term in (high, taps - high):
        spread = pltpu.roll(jnp.broadcast_to(term, ROLL), 0, 1, stride=STRIDE, stride_axis=0)
        terms.append(spread[:ROWS, :SPAN].astype(BF16))
    fir = jnp.concatenate(terms, axis=0)

    begun = 0
    for p in range(len(PIECES)):
        raw_copies[p].wait()
        ready = sum(PIECES[p]) if p + 1 < len(PIECES) else T_PAD
        some = range(begun, (ready - SPAN) // (STRIDE * ROWS) + 1)
        begun = some.stop
        for b in some:
            span = raw[STRIDE * ROWS * b : STRIDE * ROWS * b + SPAN, :]
            both = jnp.dot(fir, span, preferred_element_type=F32)
            filt[ROWS * b : ROWS * b + ROWS, :] = (both[:ROWS] + both[ROWS:]).astype(BF16)
    for t in range(TILES):
        table_copies[t].wait()
        parts = []
        for i in range(2):
            rows = table[t, i].reshape(FT, NS // 2)
            early = jnp.dot(rows, filt[: NS // 2, :], preferred_element_type=F32)
            late = jnp.dot(rows, filt[NS // 2 : NS, :], preferred_element_type=F32)
            early = early.reshape(2, 2, HALF, CH)
            late = late.reshape(2, 2, HALF, CH)
            part = jnp.stack([early[:, 0] + late[:, 0], early[:, 1] - late[:, 1]], axis=1)
            parts += [part.reshape(2, 2, FG // BAND, BAND // 2, CH)]
        power = sum(jnp.sum(part * part, axis=(1, 3)) for part in parts) * (0.5 / BAND)
        scale = (1.0 / jnp.sqrt(power + 1e-06))[:, None, :, None, :]
        for i in range(2):
            white = (parts[i] * scale).reshape(FT, CH).T
            for h in range(2):
                some = white[:, FG * h : FG * h + FG]
                at = i * CH
                out[2 * t + h, at : at + CH, :] = some.astype(BF16)
                for k in range(CH // 64):
                    at = u * 8 + i * 4 + k
                    src[2 * t + h, at : at + 1, :] = some[64 * k : 64 * k + 1, :]
    if before:
        src[:, :8, :] = before[0][...].astype(F32)[:, :8, :]
    else:
        src[:, 8:, :] = jnp.zeros((GROUP, 8, FG), F32)
    src_ref[...] = src[...].astype(BF16)


def cross_kernel(tiles, place, *refs):
    chunks, (out, sources) = refs[:SUBS_DEV], refs[SUBS_DEV:]
    for m in range(GROUP):
        halo = chunks[-1][m, SIZE:, :].astype(F32)
        for u in range(SUBS_DEV):
            for i in range(2):
                row = m * 4 + u * 2 + i
                for k in range(4):
                    at = u * 8 + i * 4 + k
                    sources[k, row : row + 1, :] = halo[at : at + 1]
                    sources[8 + k, row : row + 1, :] = halo[16 + at : 17 + at]
                    own = chunks[u][m, i * CH + 64 * k : i * CH + 64 * k + 16, :]
                    sources[4 + k, row : row + 1, :] = own.astype(F32)[:1]

    for q in range(SLOTS):
        live = q < place[0]
        source = tiles[q, 0] - place[1] + 2
        receiver = tiles[q, 1] - place[1]

        @pl.when(live)
        def _(q=q, source=source, receiver=receiver):
            def rows(cb, carry):
                at = pl.multiple_of(receiver * TILE + cb * 32, 32)
                re = [jnp.zeros((32, FG), F32) for _ in range(VS)]
                im = [jnp.zeros((32, FG), F32) for _ in range(VS)]
                for m in range(GROUP):
                    for u in range(SUBS_DEV):
                        b_re = chunks[u][m, pl.ds(at, 32), :].astype(F32)
                        b_im = chunks[u][m, pl.ds(at + CH, 32), :].astype(F32)
                        row = m * 4 + u * 2
                        for s in range(VS):
                            a_re = sources[source * VS + s, row : row + 1, :]
                            a_im = sources[source * VS + s, row + 1 : row + 2, :]
                            re[s] = re[s] + (a_re * b_re + a_im * b_im)
                            im[s] = im[s] + (a_re * b_im - a_im * b_re)
                for s in range(VS):
                    for h in range(4):
                        both = [re[s][8 * h : 8 * h + 8], im[s][8 * h : 8 * h + 8]]
                        out[s * 16 + cb * 4 + h, q] = jnp.concatenate(both, axis=0).astype(BF16)
                return carry

            lax.fori_loop(0, TILE // 32, rows, 0)

        @pl.when(jnp.logical_not(live))
        def _(q=q):
            out[:, q] = jnp.zeros((WX * WZ, 16, FG), BF16)


def lag_kernel(total_subs, part_ref, table, out, lhs):
    scale = 2.0 / float(2.0 * F * total_subs) ** 0.5
    column = lax.broadcasted_iota(jnp.int32, (1, FG), 1)
    early = column < HALF
    sign = jnp.where(early, scale, -scale)
    first = jnp.where(column == 0, 0.5 * scale, sign)
    for q in range(SLOTS):
        for x in range(WX):
            pair = []
            for c in range(2):
                total = sum(part_ref[x * WZ + 2 * k + c, q].astype(F32) for k in range(WZ // 2))
                pair.append(total * (sign if x or c else first))
            swapped = [pltpu.roll(total, HALF, 1) for total in pair]
            sides = (
                jnp.where(early, pair[0], swapped[1]),
                jnp.where(early, swapped[0], pair[1]),
            )
            for side in range(2):
                high = sides[side].astype(BF16).astype(F32)
                for j, term in enumerate((high, sides[side] - high)):
                    for i in range(2):
                        lhs[
                            side,
                            32 * j + 8 * q : 32 * j + 8 * q + 8,
                            512 * i + FG * x : 512 * i + FG * x + FG,
                        ] = term[8 * i : 8 * i + 8, :]

    sums = []
    for side in range(2):
        rows = [table[t, i, h, side] for i in range(2) for t in range(TILES) for h in range(2)]
        rows = jnp.concatenate(rows, axis=0)
        both = jnp.dot(lhs[side].astype(BF16), rows, preferred_element_type=F32)
        sums.append(both[:32] + both[32:])
    head, tail = sums[0] + sums[1], sums[0] - sums[1]
    for q in range(SLOTS):
        out[:, q, : LAGS // 2] = head[8 * q : 8 * q + 8]
        out[:, q, LAGS // 2 :] = tail[8 * q : 8 * q + 8]


VMEM = pl.BlockSpec(memory_space=pltpu.VMEM)
SMEM = pl.BlockSpec(memory_space=pltpu.SMEM)
HBM = pl.BlockSpec(memory_space=pltpu.HBM)


def per_device(raw_strain, fir_taps, block_tiles, block_count):
    first_tile = lax.axis_index("pair") * (CH // TILE)
    place = jnp.stack([block_count[0], first_tile]).astype(jnp.int32)
    table = jnp.asarray(dft_table())

    def spectra(u, *before):
        rows = SIZE + (32 if u == SUBS_DEV - 1 else 0)
        return pl.pallas_call(
            functools.partial(spectra_kernel, u),
            out_shape=[
                jax.ShapeDtypeStruct((GROUP, rows, FG), BF16),
                jax.ShapeDtypeStruct((GROUP, 16, FG), BF16),
            ],
            in_specs=[HBM, HBM, HBM] + [VMEM] * u,
            out_specs=[VMEM, VMEM],
            scratch_shapes=[
                pltpu.VMEM((T_PAD, CH), BF16),
                pltpu.VMEM((TILES, 2, 2, 2, HALF, NS // 2), BF16),
                pltpu.VMEM((BLOCKS * ROWS, CH), BF16),
                pltpu.VMEM((GROUP, 16, FG), F32),
                pltpu.VMEM((1, TAPS), F32),
                pltpu.VMEM((1, ROLL[1]), F32),
                pltpu.SemaphoreType.DMA((9,)),
            ],
            compiler_params=pltpu.CompilerParams(vmem_limit_bytes=50 * 1024 * 1024),
            cost_estimate=pl.CostEstimate(
                flops=4_000_000_000, bytes_accessed=13_000_000, transcendentals=0
            ),
        )(fir_taps[None, :], raw_strain, table, *before)

    groups = [
        [x * WZ + 2 * k + c for x in range(WX) for c in range(2)] for k in range(WZ // 2)
    ]

    def to_bins(array):
        return lax.all_to_all(array, "win", 0, 0, axis_index_groups=groups, tiled=True)

    count = lax.axis_size("pair")
    up = [(i, i + 1) for i in range(count - 1)]
    down = [(i + 1, i) for i in range(count - 1)]
    first, sources = spectra(0)
    first = to_bins(first)
    second, sources = spectra(1, sources)
    for side, way in enumerate((up, down)):
        halo = lax.ppermute(sources, "pair", way)
        second = lax.dynamic_update_slice(second, halo, (0, SIZE + 16 * side, 0))
    first, second = lax.optimization_barrier((first, second))
    second = to_bins(second)

    partial = pl.pallas_call(
        cross_kernel,
        out_shape=jax.ShapeDtypeStruct((WX * WZ, SLOTS, 16, FG), BF16),
        in_specs=[SMEM, SMEM] + [VMEM] * SUBS_DEV,
        out_specs=VMEM,
        scratch_shapes=[pltpu.VMEM((12, 32, FG), F32)],
        compiler_params=pltpu.CompilerParams(vmem_limit_bytes=16 * 1024 * 1024),
        cost_estimate=pl.CostEstimate(
            flops=20_000_000, bytes_accessed=4_000_000, transcendentals=0
        ),
    )(block_tiles, place, first, second)

    parts = lax.all_to_all(partial, "win", 0, 0, tiled=True)

    return pl.pallas_call(
        functools.partial(lag_kernel, SUBS_DEV * lax.axis_size("win")),
        out_shape=jax.ShapeDtypeStruct((8, SLOTS, LAGS), F32),
        in_specs=[VMEM, VMEM],
        out_specs=VMEM,
        scratch_shapes=[pltpu.VMEM((2, 64, F), F32)],
        compiler_params=pltpu.CompilerParams(vmem_limit_bytes=16 * 1024 * 1024),
        cost_estimate=pl.CostEstimate(
            flops=300_000_000, bytes_accessed=6_000_000, transcendentals=0
        ),
    )(parts, table)


def solution(mesh):
    return jax.shard_map(
        per_device,
        mesh=mesh,
        in_specs=(P("win", None, "pair"), P(), P("pair", None), P("pair")),
        out_specs=P("win", "pair", None),
        check_vma=False,
    )
```

```python
import functools

import jax
import jax.numpy as jnp
import ml_dtypes
import numpy as np
from jax import lax
from jax.experimental import pallas as pl
from jax.experimental.pallas import tpu as pltpu
from jax.sharding import PartitionSpec as P

TILE = 128
VS = 2
NS = 2048
TAPS = 64
STRIDE = 4
BAND = 64
F = 1024
LAGS = 2048
T_RAW = 8256
CH = 256
SLOTS = 4
SUBS_DEV = 2
WX = 4
WZ = 8
GROUP = 8
FG = F // GROUP
HALF = FG // 2
TILES = 4
FT = F // TILES
ROWS = 48
SPAN = 256
BLOCKS = -(-NS // ROWS)
T_PAD = (BLOCKS - 1) * STRIDE * ROWS + SPAN
ROLL = (128, 640)
SIZE = 2 * CH
PIECES = ((0, 2112), (2112, 2048), (4160, 2048), (6208, 2048))
F32 = jnp.float32
BF16 = jnp.bfloat16


def dft_table():
    freq = np.arange(F).reshape(TILES, 2, HALF, 2).transpose(0, 1, 3, 2)
    phase = freq[..., None] * np.arange(NS // 2) % NS
    angle = phase.astype(np.float32) * np.float32(2.0 * np.pi / NS)
    table = np.stack([np.cos(angle), -np.sin(angle)], axis=1)
    return table.astype(np.float32).astype(ml_dtypes.bfloat16)


def spectra_kernel(u, taps_hbm, raw_hbm, table_hbm, *refs):
    before = refs[:u]
    out_hbm, src_ref, out, raw, table, filt, src, taps_ref, row, sems = refs[u:]
    taps_copy = pltpu.make_async_copy(taps_hbm, taps_ref, sems.at[8])
    raw_copies = [
        pltpu.make_async_copy(raw_hbm.at[u, pl.ds(at, size)], raw.at[pl.ds(at, size)], sems.at[p])
        for p, (at, size) in enumerate(PIECES)
    ]
    table_copies = [
        pltpu.make_async_copy(table_hbm.at[t], table.at[t], sems.at[4 + t])
        for t in range(TILES)
    ]
    taps_copy.start()
    out_copies = [
        pltpu.make_async_copy(
            out.at[pl.ds(2 * t, 2)], out_hbm.at[pl.ds(2 * t, 2), pl.ds(0, SIZE)], sems.at[9 + t]
        )
        for t in range(TILES)
    ]
    for copy in raw_copies:
        copy.start()
    raw[T_RAW:, :] = jnp.zeros((T_PAD - T_RAW, CH), BF16)

    row[...] = jnp.zeros(row.shape, F32)
    taps_copy.wait()
    row[:, :TAPS] = taps_ref[...]
    taps = row[...]
    high = taps.astype(BF16).astype(F32)
    terms = []
    for term in (high, taps - high):
        spread = pltpu.roll(jnp.broadcast_to(term, ROLL), 0, 1, stride=STRIDE, stride_axis=0)
        terms.append(spread[:ROWS, :SPAN].astype(BF16))
    fir = jnp.concatenate(terms, axis=0)

    begun = 0
    for p in range(len(PIECES)):
        raw_copies[p].wait()
        table_copies[p].start()
        ready = sum(PIECES[p]) if p + 1 < len(PIECES) else T_PAD
        some = range(begun, (ready - SPAN) // (STRIDE * ROWS) + 1)
        begun = some.stop
        for b in some:
            span = raw[STRIDE * ROWS * b : STRIDE * ROWS * b + SPAN, :]
            both = jnp.dot(fir, span, preferred_element_type=F32)
            filt[ROWS * b : ROWS * b + ROWS, :] = (both[:ROWS] + both[ROWS:]).astype(BF16)
    for t in range(TILES):
        table_copies[t].wait()
        parts = []
        for i in range(2):
            rows = table[t, i].reshape(FT, NS // 2)
            early = jnp.dot(rows, filt[: NS // 2, :], preferred_element_type=F32)
            late = jnp.dot(rows, filt[NS // 2 : NS, :], preferred_element_type=F32)
            early = early.reshape(2, 2, HALF, CH)
            late = late.reshape(2, 2, HALF, CH)
            part = jnp.stack([early[:, 0] + late[:, 0], early[:, 1] - late[:, 1]], axis=1)
            parts += [part.reshape(2, 2, FG // BAND, BAND // 2, CH)]
        power = sum(jnp.sum(part * part, axis=(1, 3)) for part in parts) * (0.5 / BAND)
        scale = (1.0 / jnp.sqrt(power + 1e-06))[:, None, :, None, :]
        for i in range(2):
            white = (parts[i] * scale).reshape(FT, CH).T
            for h in range(2):
                some = white[:, FG * h : FG * h + FG]
                at = i * CH
                out[2 * t + h, at : at + CH, :] = some.astype(BF16)
                for k in range(CH // 64):
                    at = u * 8 + i * 4 + k
                    src[2 * t + h, at : at + 1, :] = some[64 * k : 64 * k + 1, :]
        out_copies[t].start()
    if before:
        src[:, :8, :] = before[0][...].astype(F32)[:, :8, :]
    else:
        src[:, 8:, :] = jnp.zeros((GROUP, 8, FG), F32)
    src_ref[...] = src[...].astype(BF16)
    for copy in out_copies:
        copy.wait()


def cross_kernel(tiles, place, *refs):
    chunks, (out, sources) = refs[:SUBS_DEV], refs[SUBS_DEV:]
    for m in range(GROUP):
        halo = chunks[-1][m, SIZE:, :].astype(F32)
        for u in range(SUBS_DEV):
            for i in range(2):
                row = m * 4 + u * 2 + i
                for k in range(4):
                    at = u * 8 + i * 4 + k
                    sources[k, row : row + 1, :] = halo[at : at + 1]
                    sources[8 + k, row : row + 1, :] = halo[16 + at : 17 + at]
                    own = chunks[u][m, i * CH + 64 * k : i * CH + 64 * k + 16, :]
                    sources[4 + k, row : row + 1, :] = own.astype(F32)[:1]

    for q in range(SLOTS):
        live = q < place[0]
        source = tiles[q, 0] - place[1] + 2
        receiver = tiles[q, 1] - place[1]

        @pl.when(live)
        def _(q=q, source=source, receiver=receiver):
            def rows(cb, carry):
                at = pl.multiple_of(receiver * TILE + cb * 32, 32)
                re = [jnp.zeros((32, FG), F32) for _ in range(VS)]
                im = [jnp.zeros((32, FG), F32) for _ in range(VS)]
                for m in range(GROUP):
                    for u in range(SUBS_DEV):
                        b_re = chunks[u][m, pl.ds(at, 32), :].astype(F32)
                        b_im = chunks[u][m, pl.ds(at + CH, 32), :].astype(F32)
                        row = m * 4 + u * 2
                        for s in range(VS):
                            a_re = sources[source * VS + s, row : row + 1, :]
                            a_im = sources[source * VS + s, row + 1 : row + 2, :]
                            re[s] = re[s] + (a_re * b_re + a_im * b_im)
                            im[s] = im[s] + (a_re * b_im - a_im * b_re)
                for s in range(VS):
                    for h in range(4):
                        both = [re[s][8 * h : 8 * h + 8], im[s][8 * h : 8 * h + 8]]
                        out[s * 16 + cb * 4 + h, q] = jnp.concatenate(both, axis=0).astype(BF16)
                return carry

            lax.fori_loop(0, TILE // 32, rows, 0)

        @pl.when(jnp.logical_not(live))
        def _(q=q):
            out[:, q] = jnp.zeros((WX * WZ, 16, FG), BF16)


def lag_kernel(total_subs, part_ref, table, out, lhs):
    scale = 2.0 / float(2.0 * F * total_subs) ** 0.5
    column = lax.broadcasted_iota(jnp.int32, (1, FG), 1)
    early = column < HALF
    sign = jnp.where(early, scale, -scale)
    first = jnp.where(column == 0, 0.5 * scale, sign)
    for q in range(SLOTS):
        for x in range(WX):
            pair = []
            for c in range(2):
                total = sum(part_ref[x * WZ + 2 * k + c, q].astype(F32) for k in range(WZ // 2))
                pair.append(total * (sign if x or c else first))
            swapped = [pltpu.roll(total, HALF, 1) for total in pair]
            sides = (
                jnp.where(early, pair[0], swapped[1]),
                jnp.where(early, swapped[0], pair[1]),
            )
            for side in range(2):
                high = sides[side].astype(BF16).astype(F32)
                for j, term in enumerate((high, sides[side] - high)):
                    for i in range(2):
                        lhs[
                            side,
                            32 * j + 8 * q : 32 * j + 8 * q + 8,
                            512 * i + FG * x : 512 * i + FG * x + FG,
                        ] = term[8 * i : 8 * i + 8, :]

    sums = []
    for side in range(2):
        rows = [table[t, i, h, side] for i in range(2) for t in range(TILES) for h in range(2)]
        rows = jnp.concatenate(rows, axis=0)
        both = jnp.dot(lhs[side].astype(BF16), rows, preferred_element_type=F32)
        sums.append(both[:32] + both[32:])
    head, tail = sums[0] + sums[1], sums[0] - sums[1]
    for q in range(SLOTS):
        out[:, q, : LAGS // 2] = head[8 * q : 8 * q + 8]
        out[:, q, LAGS // 2 :] = tail[8 * q : 8 * q + 8]


VMEM = pl.BlockSpec(memory_space=pltpu.VMEM)
SMEM = pl.BlockSpec(memory_space=pltpu.SMEM)
HBM = pl.BlockSpec(memory_space=pltpu.HBM)


def per_device(raw_strain, fir_taps, block_tiles, block_count):
    first_tile = lax.axis_index("pair") * (CH // TILE)
    place = jnp.stack([block_count[0], first_tile]).astype(jnp.int32)
    table = jnp.asarray(dft_table())

    def spectra(u, *before):
        rows = SIZE + (32 if u == SUBS_DEV - 1 else 0)
        return pl.pallas_call(
            functools.partial(spectra_kernel, u),
            out_shape=[
                jax.ShapeDtypeStruct((GROUP, rows, FG), BF16),
                jax.ShapeDtypeStruct((GROUP, 16, FG), BF16),
            ],
            in_specs=[HBM, HBM, HBM] + [VMEM] * u,
            out_specs=[HBM, VMEM],
            scratch_shapes=[
                pltpu.VMEM((GROUP, SIZE, FG), BF16),
                pltpu.VMEM((T_PAD, CH), BF16),
                pltpu.VMEM((TILES, 2, 2, 2, HALF, NS // 2), BF16),
                pltpu.VMEM((BLOCKS * ROWS, CH), BF16),
                pltpu.VMEM((GROUP, 16, FG), F32),
                pltpu.VMEM((1, TAPS), F32),
                pltpu.VMEM((1, ROLL[1]), F32),
                pltpu.SemaphoreType.DMA((9 + TILES,)),
            ],
            compiler_params=pltpu.CompilerParams(vmem_limit_bytes=50 * 1024 * 1024),
            cost_estimate=pl.CostEstimate(
                flops=4_000_000_000, bytes_accessed=13_000_000, transcendentals=0
            ),
        )(fir_taps[None, :], raw_strain, table, *before)

    groups = [
        [x * WZ + 2 * k + c for x in range(WX) for c in range(2)] for k in range(WZ // 2)
    ]

    def to_bins(array):
        return lax.all_to_all(array, "win", 0, 0, axis_index_groups=groups, tiled=True)

    count = lax.axis_size("pair")
    up = [(i, i + 1) for i in range(count - 1)]
    down = [(i + 1, i) for i in range(count - 1)]
    first, sources = spectra(0)
    first = to_bins(first)
    second, sources = spectra(1, sources)
    for side, way in enumerate((up, down)):
        halo = lax.ppermute(sources, "pair", way)
        second = lax.dynamic_update_slice(second, halo, (0, SIZE + 16 * side, 0))
    second = to_bins(second)

    partial = pl.pallas_call(
        cross_kernel,
        out_shape=jax.ShapeDtypeStruct((WX * WZ, SLOTS, 16, FG), BF16),
        in_specs=[SMEM, SMEM] + [VMEM] * SUBS_DEV,
        out_specs=VMEM,
        scratch_shapes=[pltpu.VMEM((12, 32, FG), F32)],
        compiler_params=pltpu.CompilerParams(vmem_limit_bytes=16 * 1024 * 1024),
        cost_estimate=pl.CostEstimate(
            flops=20_000_000, bytes_accessed=4_000_000, transcendentals=0
        ),
    )(block_tiles, place, first, second)

    parts = lax.all_to_all(partial, "win", 0, 0, tiled=True)

    return pl.pallas_call(
        functools.partial(lag_kernel, SUBS_DEV * lax.axis_size("win")),
        out_shape=jax.ShapeDtypeStruct((8, SLOTS, LAGS), F32),
        in_specs=[VMEM, VMEM],
        out_specs=VMEM,
        scratch_shapes=[pltpu.VMEM((2, 64, F), F32)],
        compiler_params=pltpu.CompilerParams(vmem_limit_bytes=16 * 1024 * 1024),
        cost_estimate=pl.CostEstimate(
            flops=300_000_000, bytes_accessed=6_000_000, transcendentals=0
        ),
    )(parts, table)


def solution(mesh):
    return jax.shard_map(
        per_device,
        mesh=mesh,
        in_specs=(P("win", None, "pair"), P(), P("pair", None), P("pair")),
        out_specs=P("win", "pair", None),
        check_vma=False,
    )
```

```python
import functools

import jax
import jax.numpy as jnp
import ml_dtypes
import numpy as np
from jax import lax
from jax.experimental import pallas as pl
from jax.experimental.pallas import tpu as pltpu
from jax.sharding import PartitionSpec as P

TILE = 128
VS = 2
NS = 2048
TAPS = 64
STRIDE = 4
BAND = 64
F = 1024
LAGS = 2048
T_RAW = 8256
CH = 256
SLOTS = 4
SUBS_DEV = 2
WX = 4
WZ = 8
GROUP = 8
FG = F // GROUP
HALF = FG // 2
TILES = 4
FT = F // TILES
ROWS = 48
SPAN = 256
BLOCKS = -(-NS // ROWS)
T_PAD = (BLOCKS - 1) * STRIDE * ROWS + SPAN
ROLL = (128, 640)
SIZE = 2 * CH
PIECES = ((0, 2112), (2112, 2048), (4160, 2048), (6208, 2048))
F32 = jnp.float32
BF16 = jnp.bfloat16


def dft_table():
    freq = np.arange(F).reshape(TILES, 2, HALF, 2).transpose(0, 1, 3, 2)
    phase = freq[..., None] * np.arange(NS // 2) % NS
    angle = phase.astype(np.float32) * np.float32(2.0 * np.pi / NS)
    table = np.stack([np.cos(angle), -np.sin(angle)], axis=1)
    return table.astype(np.float32).astype(ml_dtypes.bfloat16)


def spectra_kernel(u, taps_hbm, raw_hbm, table_hbm, *refs):
    out_hbm, src_ref = refs[0], refs[1] if u else None
    out, raw, table, filt, src, taps_ref, row, sems = refs[1 + u :]
    taps_copy = pltpu.make_async_copy(taps_hbm, taps_ref, sems.at[8])
    raw_copies = [
        pltpu.make_async_copy(raw_hbm.at[u, pl.ds(at, size)], raw.at[pl.ds(at, size)], sems.at[p])
        for p, (at, size) in enumerate(PIECES)
    ]
    table_copies = [
        pltpu.make_async_copy(table_hbm.at[t], table.at[t], sems.at[4 + t])
        for t in range(TILES)
    ]
    taps_copy.start()
    out_copies = [
        pltpu.make_async_copy(
            out.at[pl.ds(2 * t, 2)], out_hbm.at[pl.ds(2 * t, 2), pl.ds(0, SIZE)], sems.at[9 + t]
        )
        for t in range(TILES)
    ]
    for copy in raw_copies:
        copy.start()
    raw[T_RAW:, :] = jnp.zeros((T_PAD - T_RAW, CH), BF16)

    row[...] = jnp.zeros(row.shape, F32)
    taps_copy.wait()
    row[:, :TAPS] = taps_ref[...]
    taps = row[...]
    high = taps.astype(BF16).astype(F32)
    terms = []
    for term in (high, taps - high):
        spread = pltpu.roll(jnp.broadcast_to(term, ROLL), 0, 1, stride=STRIDE, stride_axis=0)
        terms.append(spread[:ROWS, :SPAN].astype(BF16))
    fir = jnp.concatenate(terms, axis=0)

    begun = 0
    for p in range(len(PIECES)):
        raw_copies[p].wait()
        table_copies[p].start()
        ready = sum(PIECES[p]) if p + 1 < len(PIECES) else T_PAD
        some = range(begun, (ready - SPAN) // (STRIDE * ROWS) + 1)
        begun = some.stop
        for b in some:
            span = raw[STRIDE * ROWS * b : STRIDE * ROWS * b + SPAN, :]
            both = jnp.dot(fir, span, preferred_element_type=F32)
            filt[ROWS * b : ROWS * b + ROWS, :] = (both[:ROWS] + both[ROWS:]).astype(BF16)
    for t in range(TILES):
        table_copies[t].wait()
        parts = []
        for i in range(2):
            rows = table[t, i].reshape(FT, NS // 2)
            early = jnp.dot(rows, filt[: NS // 2, :], preferred_element_type=F32)
            late = jnp.dot(rows, filt[NS // 2 : NS, :], preferred_element_type=F32)
            early = early.reshape(2, 2, HALF, CH)
            late = late.reshape(2, 2, HALF, CH)
            part = jnp.stack([early[:, 0] + late[:, 0], early[:, 1] - late[:, 1]], axis=1)
            parts += [part.reshape(2, 2, FG // BAND, BAND // 2, CH)]
        power = sum(jnp.sum(part * part, axis=(1, 3)) for part in parts) * (0.5 / BAND)
        scale = (1.0 / jnp.sqrt(power + 1e-06))[:, None, :, None, :]
        for i in range(2):
            white = (parts[i] * scale).reshape(FT, CH).T
            for h in range(2):
                some = white[:, FG * h : FG * h + FG]
                at = i * CH
                out[2 * t + h, at : at + CH, :] = some.astype(BF16)
                for k in range(CH // 64 if u else 0):
                    at = i * 4 + k
                    src[2 * t + h, at : at + 1, :] = some[64 * k : 64 * k + 1, :]
        out_copies[t].start()
    if u:
        src[:, 8:, :] = jnp.zeros((GROUP, 8, FG), F32)
        src_ref[...] = src[...].astype(BF16)
    for copy in out_copies:
        copy.wait()


def source_kernel(chunk, out, rows):
    rows[:, 8:, :] = jnp.zeros((GROUP, 8, FG), F32)
    for m in range(GROUP):
        for i in range(2):
            for k in range(4):
                own = chunk[m, i * CH + 64 * k : i * CH + 64 * k + 16, :].astype(F32)
                rows[m, i * 4 + k : i * 4 + k + 1, :] = own[:1]
    out[...] = rows[...].astype(BF16)


def cross_kernel(u, tiles, place, chunk, *refs):
    others, (out, sources) = refs[:-2], refs[-2:]
    before = others if u else ()
    for m in range(GROUP):
        if u:
            halo = chunk[m, SIZE:, :].astype(F32)
            left, right = halo[:16], halo[16:]
        else:
            left, right = (other[m].astype(F32) for other in others)
        for i in range(2):
            row = m * 2 + i
            for k in range(4):
                at = i * 4 + k
                sources[k, row : row + 1, :] = left[at : at + 1]
                sources[8 + k, row : row + 1, :] = right[at : at + 1]
                own = chunk[m, i * CH + 64 * k : i * CH + 64 * k + 16, :]
                sources[4 + k, row : row + 1, :] = own.astype(F32)[:1]

    for q in range(SLOTS):
        live = q < place[0]
        source = tiles[q, 0] - place[1] + 2
        receiver = tiles[q, 1] - place[1]

        @pl.when(live)
        def _(q=q, source=source, receiver=receiver):
            def rows(cb, carry):
                at = pl.multiple_of(receiver * TILE + cb * 32, 32)
                re = [jnp.zeros((32, FG), F32) for _ in range(VS)]
                im = [jnp.zeros((32, FG), F32) for _ in range(VS)]
                for m in range(GROUP):
                    b_re = chunk[m, pl.ds(at, 32), :].astype(F32)
                    b_im = chunk[m, pl.ds(at + CH, 32), :].astype(F32)
                    row = m * 2
                    for s in range(VS):
                        a_re = sources[source * VS + s, row : row + 1, :]
                        a_im = sources[source * VS + s, row + 1 : row + 2, :]
                        re[s] = re[s] + (a_re * b_re + a_im * b_im)
                        im[s] = im[s] + (a_re * b_im - a_im * b_re)
                for s in range(VS):
                    for h in range(4):
                        both = [re[s][8 * h : 8 * h + 8], im[s][8 * h : 8 * h + 8]]
                        both = jnp.concatenate(both, axis=0)
                        owner = s * 16 + cb * 4 + h
                        if before:
                            both = both + before[0][owner, q]
                        out[owner, q] = both.astype(out.dtype)
                return carry

            lax.fori_loop(0, TILE // 32, rows, 0)

        @pl.when(jnp.logical_not(live))
        def _(q=q):
            out[:, q] = jnp.zeros((WX * WZ, 16, FG), out.dtype)


def lag_kernel(total_subs, part_ref, table, out, lhs):
    scale = 2.0 / float(2.0 * F * total_subs) ** 0.5
    column = lax.broadcasted_iota(jnp.int32, (1, FG), 1)
    early = column < HALF
    sign = jnp.where(early, scale, -scale)
    first = jnp.where(column == 0, 0.5 * scale, sign)
    for q in range(SLOTS):
        for x in range(WX):
            pair = []
            for c in range(2):
                total = sum(part_ref[x * WZ + 2 * k + c, q].astype(F32) for k in range(WZ // 2))
                pair.append(total * (sign if x or c else first))
            swapped = [pltpu.roll(total, HALF, 1) for total in pair]
            sides = (
                jnp.where(early, pair[0], swapped[1]),
                jnp.where(early, swapped[0], pair[1]),
            )
            for side in range(2):
                high = sides[side].astype(BF16).astype(F32)
                for j, term in enumerate((high, sides[side] - high)):
                    for i in range(2):
                        lhs[
                            side,
                            32 * j + 8 * q : 32 * j + 8 * q + 8,
                            512 * i + FG * x : 512 * i + FG * x + FG,
                        ] = term[8 * i : 8 * i + 8, :]

    sums = []
    for side in range(2):
        rows = [table[t, i, h, side] for i in range(2) for t in range(TILES) for h in range(2)]
        rows = jnp.concatenate(rows, axis=0)
        both = jnp.dot(lhs[side].astype(BF16), rows, preferred_element_type=F32)
        sums.append(both[:32] + both[32:])
    head, tail = sums[0] + sums[1], sums[0] - sums[1]
    for q in range(SLOTS):
        out[:, q, : LAGS // 2] = head[8 * q : 8 * q + 8]
        out[:, q, LAGS // 2 :] = tail[8 * q : 8 * q + 8]


VMEM = pl.BlockSpec(memory_space=pltpu.VMEM)
SMEM = pl.BlockSpec(memory_space=pltpu.SMEM)
HBM = pl.BlockSpec(memory_space=pltpu.HBM)


def per_device(raw_strain, fir_taps, block_tiles, block_count):
    first_tile = lax.axis_index("pair") * (CH // TILE)
    place = jnp.stack([block_count[0], first_tile]).astype(jnp.int32)
    table = jnp.asarray(dft_table())

    def spectra(u):
        rows = SIZE + (32 if u == SUBS_DEV - 1 else 0)
        return pl.pallas_call(
            functools.partial(spectra_kernel, u),
            out_shape=[
                jax.ShapeDtypeStruct((GROUP, rows, FG), BF16),
                jax.ShapeDtypeStruct((GROUP, 16, FG), BF16),
            ][: 1 + u],
            in_specs=[HBM, HBM, HBM],
            out_specs=[HBM, VMEM][: 1 + u],
            scratch_shapes=[
                pltpu.VMEM((GROUP, SIZE, FG), BF16),
                pltpu.VMEM((T_PAD, CH), BF16),
                pltpu.VMEM((TILES, 2, 2, 2, HALF, NS // 2), BF16),
                pltpu.VMEM((BLOCKS * ROWS, CH), BF16),
                pltpu.VMEM((GROUP, 16, FG), F32),
                pltpu.VMEM((1, TAPS), F32),
                pltpu.VMEM((1, ROLL[1]), F32),
                pltpu.SemaphoreType.DMA((9 + TILES,)),
            ],
            compiler_params=pltpu.CompilerParams(vmem_limit_bytes=50 * 1024 * 1024),
            cost_estimate=pl.CostEstimate(
                flops=4_000_000_000, bytes_accessed=13_000_000, transcendentals=0
            ),
        )(fir_taps[None, :], raw_strain, table)

    groups = [
        [x * WZ + 2 * k + c for x in range(WX) for c in range(2)] for k in range(WZ // 2)
    ]

    def to_bins(array):
        return lax.all_to_all(array, "win", 0, 0, axis_index_groups=groups, tiled=True)

    count = lax.axis_size("pair")
    up = [(i, i + 1) for i in range(count - 1)]
    down = [(i + 1, i) for i in range(count - 1)]

    def both_ways(sources):
        return [lax.ppermute(sources, "pair", way) for way in (up, down)]

    def cross(u, chunk, *others):
        return pl.pallas_call(
            functools.partial(cross_kernel, u),
            out_shape=jax.ShapeDtypeStruct((WX * WZ, SLOTS, 16, FG), BF16 if u else F32),
            in_specs=[SMEM, SMEM] + [VMEM] * (1 + len(others)),
            out_specs=VMEM,
            scratch_shapes=[pltpu.VMEM((12, 16, FG), F32)],
            compiler_params=pltpu.CompilerParams(vmem_limit_bytes=16 * 1024 * 1024),
            cost_estimate=pl.CostEstimate(
                flops=10_000_000, bytes_accessed=4_000_000, transcendentals=0
            ),
        )(block_tiles, place, chunk, *others)

    first = to_bins(spectra(0)[0])
    second, sources = spectra(1)
    for side, halo in enumerate(both_ways(sources)):
        second = lax.dynamic_update_slice(second, halo, (0, SIZE + 16 * side, 0))
    second = to_bins(second)

    sources = pl.pallas_call(
        source_kernel,
        out_shape=jax.ShapeDtypeStruct((GROUP, 16, FG), BF16),
        in_specs=[VMEM],
        out_specs=VMEM,
        scratch_shapes=[pltpu.VMEM((GROUP, 16, FG), F32)],
    )(first)
    partial = cross(0, first, *both_ways(sources))
    partial = cross(1, second, partial)

    parts = lax.all_to_all(partial, "win", 0, 0, tiled=True)

    return pl.pallas_call(
        functools.partial(lag_kernel, SUBS_DEV * lax.axis_size("win")),
        out_shape=jax.ShapeDtypeStruct((8, SLOTS, LAGS), F32),
        in_specs=[VMEM, VMEM],
        out_specs=VMEM,
        scratch_shapes=[pltpu.VMEM((2, 64, F), F32)],
        compiler_params=pltpu.CompilerParams(vmem_limit_bytes=16 * 1024 * 1024),
        cost_estimate=pl.CostEstimate(
            flops=300_000_000, bytes_accessed=6_000_000, transcendentals=0
        ),
    )(parts, table)


def solution(mesh):
    return jax.shard_map(
        per_device,
        mesh=mesh,
        in_specs=(P("win", None, "pair"), P(), P("pair", None), P("pair")),
        out_specs=P("win", "pair", None),
        check_vma=False,
    )
```
